256 devices in a mesh: rep: 16 (over y, z_lo, core), fsdp: 16 (over z_hi, x).
Axes of the slice: x: 4, y: 4, z: 8 (z_hi: 4, z_lo: 2; z = z_hi * 2 + z_lo), core: 2. Of those that a mesh axis runs over, the one named last changes fastest.
Arguments:
- clip_tokens: bfloat16 [32768, 6144], P(('rep', 'fsdp')), may hold values from -6 to 6
- frame_ids: int32 [32768], P(('rep', 'fsdp')), may hold values from 0 to 15
- modulation: float32 [16, 6144], replicated, may hold values from -3 to 3
- query_gain: float32 [128], replicated, may hold values from 0.1 to 1.9
- query_weight: bfloat16 [16, 6144, 3072], P('rep', 'fsdp'), may hold values from -0.078125 to 0.078125
- query_cotangent: bfloat16 [32768, 3072], P(('rep', 'fsdp')), may hold values from -6 to 6
- pseudo_grad: float32 [16, 1048576], P('rep', 'fsdp'), may hold values from -6 to 6
- outer_params: float32 [1048576], P('fsdp'), may hold values from -6 to 6
- outer_momentum: float32 [1048576], P('fsdp'), may hold values from -3 to 3
Outputs:
- input_grad: bfloat16 [32768, 6144], P(('rep', 'fsdp'))
- weight_grad: bfloat16 [16, 6144, 3072], P('rep', 'fsdp')
- table_grad: float32 [16, 16, 6144], P('rep', None, 'fsdp')
- new_fragment: float32 [1048576], P('fsdp')
- new_momentum: float32 [1048576], P('fsdp')
The draws below stay inside these ranges and needn't reach their ends.
All inputs are finite; a program needn't handle non-finite values.
Results may differ from the reference program's by a relative error of at most 0.02.
Values may be sent and summed in bfloat16 or wider, within the bound.
No kernel may reach another device: no remote copies, remote signals or barrier semaphores. Data moves between devices by JAX's collectives and lax.ppermute only.
A program may use at most 128 MiB of HBM per device.

```python
import jax
import jax.numpy as jnp
from jax import lax

D = 6144
HEAD = 128
E = 3072
FRAMES = 16
TOK_DEV = 128
ROWS = 32768
FRAG = 1048576
N_REP = 16
N_FSDP = 16


def touch_ends(drawn, stream_key, least, largest):
    index_at = [jax.random.randint(jax.random.fold_in(stream_key, axis), (), 0, length) for axis, length in enumerate(drawn.shape)]
    widest = drawn.shape.index(max(drawn.shape))
    neighbour = index_at[:widest] + [(index_at[widest] + 1) % drawn.shape[widest]] + index_at[widest + 1:]
    return drawn.at[tuple(index_at)].set(least).at[tuple(neighbour)].set(largest)


def block_levels(own_key, extent, pieces, smallest, high):
    gain = 1.0
    for position, parts in pieces:
        heights = jax.random.uniform(jax.random.fold_in(jax.random.fold_in(own_key, 6), position), (parts,), jnp.float32, smallest / len(pieces), high / len(pieces))
        gain = gain * jnp.repeat(jnp.exp(heights), extent[position] // parts).reshape((-1,) + (1,) * (len(extent) - 1 - position))
    return gain


def centred(stream_key, shape, deviation, bound, pieces=(), held_as=jnp.bfloat16):
    gain = block_levels(stream_key, shape, pieces, -0.22, 0.18) if pieces else 1.0
    drawn = jax.random.normal(stream_key, shape, jnp.float32) * deviation * gain
    return jnp.minimum(jnp.maximum(drawn, -bound), bound).astype(held_as)


def setup_inputs(seed: int = 0) -> dict:
    key_list = jax.random.split(jax.random.key(seed), 10)
    return {
        "clip_tokens": centred(key_list[0], (ROWS, D), 1.0, 6.0, ((0, 256),)),
        "frame_ids": touch_ends(jax.random.randint(key_list[1], (ROWS,), 0, FRAMES), jax.random.fold_in(key_list[1], 1), 0, FRAMES - 1).astype(jnp.int32),
        "modulation": centred(key_list[2], (FRAMES, D), 0.5, 3.0, (), jnp.float32),
        "query_gain": jnp.clip(1.0 + 0.18 * jax.random.normal(key_list[3], (HEAD,), jnp.float32), 0.1, 1.9),
        "query_weight": centred(key_list[4], (N_REP, D, E), D ** -0.5, 0.078125, ((0, 16), (1, 16))),
        "query_cotangent": centred(key_list[5], (ROWS, E), 1.0, 6.0, ((0, 256),)),
        "pseudo_grad": centred(key_list[6], (N_REP, FRAG), 1.0, 6.0, ((0, 16), (1, 16)), jnp.float32),
        "outer_params": centred(key_list[7], (FRAG,), 1.0, 6.0, ((0, 16),), jnp.float32),
        "outer_momentum": centred(key_list[8], (FRAG,), 0.5, 3.0, ((0, 16),), jnp.float32),
    }


EPSILON = 1e-06
OUTER_RATE = 0.7
OUTER_MOMENTUM = 0.9

def replica_backward(operands):
    tokens, frames, modulation, query_gain, weight, cotangent = operands
    rows_all = tokens.shape[0]
    tokens_f = tokens.astype(jnp.float32)
    inverse = lax.rsqrt(lax.optimization_barrier(jnp.mean(tokens_f * tokens_f, axis=-1, keepdims=True)) + EPSILON)
    normed = tokens_f * inverse
    frame_mod = modulation[frames]
    normal_in = (normed * (1.0 + frame_mod)).astype(jnp.bfloat16)
    width_part = D // N_FSDP
    blocks = normal_in.reshape(rows_all, N_FSDP, width_part).transpose(1, 0, 2)
    weight_blocks = weight.reshape(N_FSDP, width_part, E)

    def add_block(total, pair):
        partial_sum = jnp.dot(pair[0], pair[1], preferred_element_type=jnp.float32).astype(jnp.bfloat16)
        partial_sum = lax.optimization_barrier(partial_sum)
        return (total + partial_sum.astype(jnp.float32), None)
    projected, unused = lax.scan(add_block, jnp.zeros((rows_all, E), jnp.float32), (blocks, weight_blocks))
    heads = projected.reshape(rows_all, E // HEAD, HEAD)
    head_inv = lax.rsqrt(lax.optimization_barrier(jnp.mean(heads * heads, axis=-1, keepdims=True)) + EPSILON)
    head_hat = heads * head_inv
    scaled = cotangent.astype(jnp.float32).reshape(rows_all, E // HEAD, HEAD) * query_gain
    head_grad = head_inv * (scaled - head_hat * lax.optimization_barrier(jnp.mean(scaled * head_hat, axis=-1, keepdims=True)))
    proj_grad = head_grad.reshape(rows_all, E).astype(jnp.bfloat16)
    weight_grad = lax.dot_general(normal_in, proj_grad, (((0,), (0,)), ((), ())), preferred_element_type=jnp.float32).astype(jnp.bfloat16)
    normal_grad = lax.dot_general(proj_grad, weight, (((1,), (1,)), ((), ())), preferred_element_type=jnp.float32).astype(jnp.bfloat16)
    normal_grad = lax.optimization_barrier(normal_grad).astype(jnp.float32)
    table_grad = jax.ops.segment_sum(normal_grad * normed, frames, num_segments=FRAMES)
    grad_hat = normal_grad * (1.0 + frame_mod)
    input_grad = inverse * (grad_hat - normed * lax.optimization_barrier(jnp.mean(grad_hat * normed, axis=-1, keepdims=True)))
    return (input_grad.astype(jnp.bfloat16), weight_grad, table_grad)

def reference(clip_tokens, frame_ids, modulation, query_gain, query_weight, query_cotangent, pseudo_grad, outer_params, outer_momentum):
    group_rows = TOK_DEV * N_FSDP
    token_groups = clip_tokens.reshape(N_REP, group_rows, D)
    frame_groups = frame_ids.reshape(N_REP, group_rows)
    grad_groups = query_cotangent.reshape(N_REP, group_rows, E)

    def one_replica(operands):
        return replica_backward((operands[0], operands[1], modulation, query_gain, operands[2], operands[3]))
    input_grad, weight_grad, table_grad = lax.map(one_replica, (token_groups, frame_groups, query_weight, grad_groups))
    average = lax.optimization_barrier(jnp.sum(pseudo_grad, axis=0)) / N_REP
    new_momentum = OUTER_MOMENTUM * outer_momentum + average
    new_fragment = outer_params - OUTER_RATE * (average + OUTER_MOMENTUM * new_momentum)
    return (input_grad.reshape(ROWS, D), weight_grad, table_grad, new_fragment, new_momentum)
```

```python
import jax
import jax.numpy as jnp
from jax import lax
from jax.sharding import Mesh
from jax.sharding import PartitionSpec as P

EPSILON = 1e-06
OUTER_RATE = 0.7
OUTER_MOMENTUM = 0.9
CHUNKS = 4
SIDE = 4


def shift(value, axis, step):
    return lax.ppermute(value, axis, [(i, (i + step) % SIDE) for i in range(SIDE)])


def exchange(value, axis, bit):
    return lax.ppermute(value, axis, [(i, i ^ bit) for i in range(16)])


def gather_ring(value, axis):
    half = value.shape[0] // 2
    left = shift(value, axis, 1)
    right = shift(value, axis, -1)
    top = shift(left[:half], axis, 1)
    bottom = shift(right[half:], axis, -1)
    return [value, left, right, jnp.concatenate([top, bottom], axis=0)]


def scatter_ring(own, to_left, to_right, opposite, axis):
    half = own.shape[0] // 2
    from_left = shift(opposite[:half], axis, 1)
    from_right = shift(opposite[half:], axis, -1)
    f32 = jnp.float32
    on_right = jnp.concatenate(
        [
            (to_right[:half].astype(f32) + from_left.astype(f32)).astype(own.dtype),
            to_right[half:],
        ],
        axis=0,
    )
    on_left = jnp.concatenate(
        [
            to_left[:half],
            (to_left[half:].astype(f32) + from_right.astype(f32)).astype(own.dtype),
        ],
        axis=0,
    )
    return own, shift(on_right, axis, 1), shift(on_left, axis, -1)


def outer_step(pseudo_grad, outer_params, outer_momentum):
    total = pseudo_grad.astype(jnp.bfloat16)
    for bit in (1, 4, 8, 2):
        other = exchange(total, "rep", bit)
        wide = total.astype(jnp.float32) + other.astype(jnp.float32)
        total = wide.astype(jnp.bfloat16)
    average = wide / 16
    new_momentum = OUTER_MOMENTUM * outer_momentum + average
    new_fragment = outer_params - OUTER_RATE * (average + OUTER_MOMENTUM * new_momentum)
    return new_fragment, new_momentum


def shards(
    clip_tokens,
    frame_ids,
    modulation,
    query_gain,
    query_weight,
    query_cotangent,
    pseudo_grad,
    outer_params,
    outer_momentum,
):
    f32 = jnp.float32
    bf16 = jnp.bfloat16
    z = lax.axis_index("zh")
    rows, width = clip_tokens.shape
    part = width // SIDE
    frame_count = modulation.shape[0]
    frames = jnp.arange(frame_count, dtype=jnp.int32)
    columns = query_weight.shape[2]
    step = columns // CHUNKS
    head = query_gain.shape[0]

    weights = [
        lax.all_gather(
            query_weight[0][:, c * step : (c + 1) * step], "xx", axis=0, tiled=True
        )
        for c in range(CHUNKS)
    ]

    def features_of(place):
        return lax.dynamic_slice_in_dim(clip_tokens, (place % SIDE) * part, part, 1)

    pieces = [
        features_of(z),
        shift(features_of(z + 1), "zh", 1),
        shift(features_of(z + 3), "zh", -1),
        shift(features_of(z + 2), "zh", 2),
    ]
    tokens_f = clip_tokens.astype(f32)
    inverse = lax.rsqrt(jnp.mean(tokens_f * tokens_f, axis=-1, keepdims=True) + EPSILON)
    marks = jnp.concatenate([inverse, frame_ids[:, None].astype(f32)], axis=1)
    all_marks = jnp.concatenate(
        [
            marks,
            shift(marks, "zh", 1),
            shift(marks, "zh", -1),
            shift(marks, "zh", 2),
        ],
        axis=0,
    )
    group_ids = all_marks[:, 1].astype(jnp.int32)
    group_hot = (group_ids[:, None] == frames[None, :]).astype(f32)
    group_mod = lax.dynamic_slice_in_dim(modulation, z * part, part, 1)
    group_normed = jnp.concatenate(pieces, axis=0).astype(f32) * all_marks[:, :1]
    normal_in = (
        group_normed
        * (1.0 + jnp.dot(group_hot, group_mod, precision=lax.Precision.HIGHEST))
    ).astype(bf16)

    normal_total = None
    weight_grads = []
    for c in range(CHUNKS):
        partial = jnp.dot(normal_in, weights[c], preferred_element_type=f32).astype(bf16)
        blocks = [partial[i * rows : (i + 1) * rows] for i in range(SIDE)]
        terms = scatter_ring(blocks[0], blocks[1], blocks[2], blocks[3], "zh")
        projected = terms[0].astype(f32) + terms[1].astype(f32) + terms[2].astype(f32)
        heads = projected.reshape(rows, step // head, head)
        head_inv = lax.rsqrt(jnp.mean(heads * heads, axis=-1, keepdims=True) + EPSILON)
        head_hat = heads * head_inv
        scaled = (
            query_cotangent[:, c * step : (c + 1) * step]
            .astype(f32)
            .reshape(rows, step // head, head)
            * query_gain
        )
        head_grad = head_inv * (
            scaled - head_hat * jnp.mean(scaled * head_hat, axis=-1, keepdims=True)
        )
        proj_grad = head_grad.reshape(rows, step).astype(bf16)
        group_grad = jnp.concatenate(gather_ring(proj_grad, "zh"), axis=0)
        term = lax.dot_general(
            group_grad, weights[c], (((1,), (1,)), ((), ())), preferred_element_type=f32
        )
        normal_total = term if normal_total is None else normal_total + term
        weight_term = lax.dot_general(
            normal_in, group_grad, (((0,), (0,)), ((), ())), preferred_element_type=f32
        ).astype(bf16)
        weight_grads.append(
            lax.psum_scatter(weight_term, "xx", scatter_dimension=0, tiled=True)
        )
    weight_grad = jnp.concatenate(weight_grads, axis=1)[None]

    group_grad = normal_total.astype(bf16)
    back = [
        group_grad[:rows],
        shift(group_grad[rows : 2 * rows], "zh", -1),
        shift(group_grad[2 * rows : 3 * rows], "zh", 1),
        shift(group_grad[3 * rows :], "zh", 2),
    ]
    local_table = lax.dot_general(
        group_hot,
        group_grad.astype(f32) * group_normed,
        (((0,), (0,)), ((), ())),
        precision=lax.Precision.HIGHEST,
    )
    table_grad = lax.psum_scatter(
        local_table, "xx", scatter_dimension=1, tiled=True
    )[None]
    normal_grad = jnp.zeros((rows, width), bf16)
    for place, piece in ((z, back[0]), (z + 1, back[1]), (z + 3, back[2]), (z + 2, back[3])):
        normal_grad = lax.dynamic_update_slice_in_dim(
            normal_grad, piece, (place % SIDE) * part, 1
        )
    normal_grad = normal_grad.astype(f32)
    normed = tokens_f * inverse
    one_hot = (frame_ids[:, None] == frames[None, :]).astype(f32)
    frame_mod = jnp.dot(one_hot, modulation, precision=lax.Precision.HIGHEST)
    grad_hat = normal_grad * (1.0 + frame_mod)
    input_grad = (
        inverse * (grad_hat - normed * jnp.mean(grad_hat * normed, axis=-1, keepdims=True))
    ).astype(bf16)
    new_fragment, new_momentum = outer_step(pseudo_grad[0], outer_params, outer_momentum)
    return (input_grad, weight_grad, table_grad, new_fragment, new_momentum)


def solution(mesh):
    grid = Mesh(mesh.devices.reshape(-1, SIDE, SIDE), ("rep", "zh", "xx"))
    fsdp = ("zh", "xx")
    every = ("rep", "zh", "xx")
    return jax.shard_map(
        shards,
        mesh=grid,
        in_specs=(
            P(every, None),
            P(every),
            P(),
            P(),
            P("rep", fsdp, None),
            P(every, None),
            P("rep", fsdp),
            P(fsdp),
            P(fsdp),
        ),
        out_specs=(
            P(every, None),
            P("rep", fsdp, None),
            P("rep", None, fsdp),
            P(fsdp),
            P(fsdp),
        ),
        check_vma=False,
    )
```

```python
import functools

import jax
import jax.numpy as jnp
from jax import lax
from jax.experimental import pallas as pl
from jax.experimental.pallas import tpu as pltpu
from jax.sharding import Mesh
from jax.sharding import PartitionSpec as P

EPSILON = 1e-06
OUTER_RATE = 0.7
OUTER_MOMENTUM = 0.9
CHUNKS = 4
SIDE = 4
F32 = jnp.float32
BF16 = jnp.bfloat16
PLACES = (0, 3, 1, 2)
NN = (((1,), (0,)), ((), ()))
NT = (((1,), (1,)), ((), ()))
TN = (((0,), (0,)), ((), ()))


def shift(value, axis, step):
    return lax.ppermute(value, axis, [(i, (i + step) % SIDE) for i in range(SIDE)])


def exchange(value, axis, bit):
    return lax.ppermute(value, axis, [(i, i ^ bit) for i in range(16)])


def call(kernel, outs, *operands, flops=0):
    size = sum(a.size * a.dtype.itemsize for a in operands) + sum(
        o.size * o.dtype.itemsize for o in outs
    )
    in_specs = [
        pl.BlockSpec(memory_space=pltpu.SMEM if a.ndim == 1 else pltpu.VMEM) for a in operands
    ]
    out_specs = [pl.BlockSpec(memory_space=pltpu.VMEM) for _ in outs]
    return pl.pallas_call(
        kernel,
        out_shape=outs,
        in_specs=in_specs,
        out_specs=out_specs,
        compiler_params=pltpu.CompilerParams(vmem_limit_bytes=40 * 1024 * 1024),
        cost_estimate=pl.CostEstimate(flops=flops, bytes_accessed=size, transcendentals=0),
    )(*operands)


def shape(rows, columns, dtype):
    return jax.ShapeDtypeStruct((rows, columns), dtype)


def gather_ring(value, axis):
    half = value.shape[0] // 2
    left = shift(value, axis, 1)
    right = shift(value, axis, -1)
    top = shift(left[:half], axis, 1)
    bottom = shift(right[half:], axis, -1)
    return [value, left, right, top, bottom]


def relay_kernel(keep_r, got_r, keep_l, got_l, out_r, out_l):
    half = keep_r.shape[0]
    out_r[...] = (keep_r[...] + got_r[:half, :].astype(F32)).astype(BF16)
    out_l[...] = (keep_l[...] + got_l[:half, :].astype(F32)).astype(BF16)


def scatter_ring(message_r, message_l, keep_r, keep_l, axis):
    half, columns = keep_r.shape
    got_r = shift(message_r, axis, 1)
    got_l = shift(message_l, axis, -1)
    relay_r, relay_l = call(
        relay_kernel, [shape(half, columns, BF16)] * 2, keep_r, got_r, keep_l, got_l
    )
    return got_r, got_l, shift(relay_r, axis, 1), shift(relay_l, axis, -1)


def sum_kernel(own, got_r, got_l, last_r, last_l, out):
    half = last_r.shape[0]
    out[:half, :] = (
        own[:half, :] + last_r[...].astype(F32) + got_l[half:, :].astype(F32)
    ).astype(out.dtype)
    out[half:, :] = (
        own[half:, :] + got_r[half:, :].astype(F32) + last_l[...].astype(F32)
    ).astype(out.dtype)


def split_out(blocks, own, message_r, message_l, keep_r, keep_l):
    half = keep_r.shape[0]
    own[...] = blocks[0]
    message_r[:half, :] = blocks[3][:half].astype(BF16)
    message_r[half:, :] = blocks[2][half:].astype(BF16)
    keep_r[...] = blocks[2][:half]
    message_l[:half, :] = blocks[3][half:].astype(BF16)
    message_l[half:, :] = blocks[1][:half].astype(BF16)
    keep_l[...] = blocks[1][half:]


def split_shapes(rows, columns):
    return [
        shape(rows, columns, F32),
        shape(rows, columns, BF16),
        shape(rows, columns, BF16),
        shape(rows // 2, columns, F32),
        shape(rows // 2, columns, F32),
    ]


def modulation_parts(modulation):
    high = modulation.astype(BF16)
    rest = modulation - high.astype(F32)
    middle = rest.astype(BF16)
    low = (rest - middle.astype(F32)).astype(BF16)
    return jnp.concatenate([high, middle, low], axis=0)


def hot(marks, copies, count):
    ids = marks[:, 1:2].astype(jnp.int32)
    places = lax.broadcasted_iota(jnp.int32, (marks.shape[0], copies * count), 1)
    return jnp.where(lax.rem(places, count) == ids, 1.0, 0.0).astype(BF16)


def prepare_kernel(p0, p1, p2, p3, m0, m1, m2, m3, modulation, out):
    rows = p0.shape[0]
    parts = modulation_parts(modulation[...])
    for i, (piece, marks) in enumerate(((p0, m0), (p1, m1), (p2, m2), (p3, m3))):
        mark = marks[...]
        frame_mod = jnp.dot(
            hot(mark, 3, modulation.shape[0]), parts, preferred_element_type=F32
        )
        normed = piece[...].astype(F32) * mark[:, 0:1]
        out[i * rows : (i + 1) * rows, :] = (normed * (1.0 + frame_mod)).astype(BF16)


def block_at(where, place, size):
    return pl.ds(pl.multiple_of(lax.rem(where[0] + place, SIDE) * size, 128), size)


def project_kernel(where, normal_in, w0, w1, w2, w3, w4, *outs):
    depth = w0.shape[0]
    rows = outs[0].shape[0]
    total = None
    for place, weight in zip(PLACES, (w0, w1, w2)):
        term = jnp.dot(
            normal_in[:, block_at(where, place, depth)], weight[...], preferred_element_type=F32
        )
        total = term if total is None else total + term
    half = depth // 2
    opposite = normal_in[:, block_at(where, 2, depth)]
    total = total + jnp.dot(opposite[:, :half], w3[...], preferred_element_type=F32)
    total = total + jnp.dot(opposite[:, half:], w4[...], preferred_element_type=F32)
    split_out([total[i * rows : (i + 1) * rows] for i in range(SIDE)], *outs)


def head_kernel(own, got_r, got_l, last_r, last_l, cotangent, gain, out):
    rows, columns = own.shape
    half = rows // 2
    head = gain.shape[1]
    for h in range(columns // head):
        span = slice(h * head, (h + 1) * head)
        for side in range(2):
            some = slice(side * half, (side + 1) * half)
            if side == 0:
                projected = (
                    own[some, span] + last_r[:, span].astype(F32) + got_l[half:, span].astype(F32)
                )
            else:
                projected = (
                    own[some, span] + got_r[half:, span].astype(F32) + last_l[:, span].astype(F32)
                )
            inverse = lax.rsqrt(
                jnp.mean(projected * projected, axis=-1, keepdims=True) + EPSILON
            )
            hat = projected * inverse
            scaled = cotangent[some, span].astype(F32) * gain[...]
            grad = inverse * (scaled - hat * jnp.mean(scaled * hat, axis=-1, keepdims=True))
            out[some, span] = grad.astype(BF16)


def normal_grad_kernel(first, last, where, g0, g1, g2, g3, g4, w0, w1, w2, w3, w4, *refs):
    depth = w0.shape[0]
    half = depth // 2
    rows = g0.shape[0]
    grad = jnp.concatenate([g0[...], g1[...], g2[...], g3[...], g4[...]], axis=0)
    if first:
        old, outs = None, refs
    else:
        old, outs = refs[0], refs[1:]
    for place, weights in zip(PLACES, ((w0,), (w1,), (w2,), (w3, w4))):
        if len(weights) == 2:
            weight = jnp.concatenate([weights[0][...], weights[1][...]], axis=0)
        else:
            weight = weights[0][...]
        span = block_at(where, place, depth)
        term = lax.dot_general(grad, weight, NT, preferred_element_type=F32)
        if not first:
            term = term + old[:, span]
        if last:
            for i in range(SIDE):
                outs[i][:, span] = term[i * rows : (i + 1) * rows].astype(BF16)
        else:
            outs[0][:, span] = term


def weight_grad_kernel(where, normal_in, g0, g1, g2, g3, g4, *outs):
    depth = outs[0].shape[0]
    grad = jnp.concatenate([g0[...], g1[...], g2[...], g3[...], g4[...]], axis=0)
    blocks = [
        lax.dot_general(
            normal_in[:, block_at(where, place, depth)], grad, TN, preferred_element_type=F32
        )
        for place in PLACES
    ]
    split_out(blocks, *outs)


def table_kernel(where, n0, n1, n2, n3, p0, p1, p2, p3, m0, m1, m2, m3, o0, o1, o2, o3, total):
    count, depth = o0.shape
    acc = None
    groups = ((n0, p0, m0), (n1, p1, m1), (n2, p2, m2), (n3, p3, m3))
    for grad, piece, marks in groups:
        mark = marks[...]
        product = grad[...].astype(F32) * (piece[...].astype(F32) * mark[:, 0:1])
        high = product.astype(BF16)
        low = (product - high.astype(F32)).astype(BF16)
        one_hot = hot(mark, 1, count)
        term = lax.dot_general(one_hot, high, TN, preferred_element_type=F32)
        term = term + lax.dot_general(one_hot, low, TN, preferred_element_type=F32)
        acc = term if acc is None else acc + term
    total[...] = acc
    for place, out in zip(PLACES, (o0, o1, o2, o3)):
        out[...] = total[:, block_at(where, place, depth)]


def input_kernel(where, tokens, marks, b0, b1, b2, b3, modulation, out):
    part = b0.shape[1]
    mark = marks[...]
    inverse = mark[:, 0:1]
    one_hot = hot(mark, 3, modulation.shape[0])
    places = (0, 1, 3, 2)

    def load(place, piece):
        span = block_at(where, place, part)
        frame_mod = jnp.dot(
            one_hot, modulation_parts(modulation[:, span]), preferred_element_type=F32
        )
        grad_hat = piece[...].astype(F32) * (1.0 + frame_mod)
        return span, grad_hat, tokens[:, span].astype(F32) * inverse

    total = 0.0
    for place, piece in zip(places, (b0, b1, b2, b3)):
        span, grad_hat, normed = load(place, piece)
        total = total + jnp.sum(grad_hat * normed, axis=-1, keepdims=True)
    mean = total / (part * SIDE)
    for place, piece in zip(places, (b0, b1, b2, b3)):
        span, grad_hat, normed = load(place, piece)
        out[:, span] = (inverse * (grad_hat - normed * mean)).astype(BF16)


def input_grad_of(where, tokens, marks, back, modulation):
    rows, width = tokens.shape
    part = width // SIDE
    tile = 32
    row_tile = lambda columns: pl.BlockSpec((tile, columns), lambda i: (i, 0))
    return pl.pallas_call(
        input_kernel,
        out_shape=shape(rows, width, BF16),
        grid=(rows // tile,),
        in_specs=[
            pl.BlockSpec(memory_space=pltpu.SMEM),
            row_tile(width),
            row_tile(2),
            row_tile(part),
            row_tile(part),
            row_tile(part),
            row_tile(part),
            pl.BlockSpec(modulation.shape, lambda i: (0, 0)),
        ],
        out_specs=row_tile(width),
        compiler_params=pltpu.CompilerParams(vmem_limit_bytes=40 * 1024 * 1024),
        cost_estimate=pl.CostEstimate(
            flops=rows * width * 12, bytes_accessed=rows * width * 6, transcendentals=0
        ),
    )(where, tokens, marks, *back, modulation)


def outer_step(pseudo_grad, outer_params, outer_momentum):
    total = pseudo_grad.astype(BF16)
    for bit in (1, 4, 8, 2):
        other = exchange(total, "rep", bit)
        wide = total.astype(F32) + other.astype(F32)
        total = wide.astype(BF16)
    average = wide / 16
    new_momentum = OUTER_MOMENTUM * outer_momentum + average
    new_fragment = outer_params - OUTER_RATE * (average + OUTER_MOMENTUM * new_momentum)
    return new_fragment, new_momentum


def spread(pieces, axis):
    return [
        pieces[0],
        shift(pieces[1], axis, -1),
        shift(pieces[2], axis, 1),
        shift(pieces[3], axis, 2),
    ]


def shards(
    clip_tokens,
    frame_ids,
    modulation,
    query_gain,
    query_weight,
    query_cotangent,
    pseudo_grad,
    outer_params,
    outer_momentum,
):
    z = lax.axis_index("zh")
    z_at = z.astype(jnp.int32)[None]
    x_at = lax.axis_index("xx").astype(jnp.int32)[None]
    rows, width = clip_tokens.shape
    part = width // SIDE
    depth = part // SIDE
    columns = query_weight.shape[2]
    step = columns // CHUNKS
    gain = query_gain[None, :]

    def features_of(place):
        return lax.dynamic_slice_in_dim(clip_tokens, lax.rem(z + place, SIDE) * part, part, 1)

    got = spread([features_of(0), features_of(3), features_of(1), features_of(2)], "zh")
    pieces = [got[0], got[2], got[1], got[3]]
    tokens_f = clip_tokens.astype(F32)
    inverse = lax.rsqrt(jnp.mean(tokens_f * tokens_f, axis=-1, keepdims=True) + EPSILON)
    mark = jnp.concatenate([inverse, frame_ids[:, None].astype(F32)], axis=1)
    got = spread([mark] * SIDE, "zh")
    marks = [got[0], got[2], got[1], got[3]]
    weights = [
        gather_ring(query_weight[0][:, c * step : (c + 1) * step], "xx") for c in range(CHUNKS)
    ]
    group_mod = lax.dynamic_slice_in_dim(modulation, z * part, part, 1)
    (normal_in,) = call(
        prepare_kernel, [shape(SIDE * rows, part, BF16)], *pieces, *marks, group_mod
    )
    matmul = 2 * SIDE * rows * part * step

    normal_total = []
    weight_grads = []
    for c in range(CHUNKS):
        own, message_r, message_l, keep_r, keep_l = call(
            project_kernel,
            split_shapes(rows, step),
            x_at,
            normal_in,
            *weights[c],
            flops=matmul,
        )
        terms = scatter_ring(message_r, message_l, keep_r, keep_l, "zh")
        (proj_grad,) = call(
            head_kernel,
            [shape(rows, step, BF16)],
            own,
            *terms,
            query_cotangent[:, c * step : (c + 1) * step],
            gain,
        )
        grads = gather_ring(proj_grad, "zh")
        first, last = c == 0, c == CHUNKS - 1
        normal_total = call(
            functools.partial(normal_grad_kernel, first, last),
            [shape(rows, part, BF16)] * SIDE if last else [shape(SIDE * rows, part, F32)],
            x_at,
            *grads,
            *weights[c],
            *normal_total,
            flops=matmul,
        )
        own, message_r, message_l, keep_r, keep_l = call(
            weight_grad_kernel,
            split_shapes(depth, step),
            x_at,
            normal_in,
            *grads,
            flops=matmul,
        )
        terms = scatter_ring(message_r, message_l, keep_r, keep_l, "xx")
        weight_grads += call(sum_kernel, [shape(depth, step, BF16)], own, *terms)
    weight_grad = jnp.concatenate(weight_grads, axis=1)[None]

    back = spread(normal_total, "zh")
    *tables, _ = call(
        table_kernel,
        [shape(modulation.shape[0], depth, F32)] * SIDE + [shape(modulation.shape[0], part, F32)],
        x_at,
        *normal_total,
        *pieces,
        *marks,
    )
    tables = spread(tables, "xx")
    table_grad = (tables[0] + tables[1] + tables[2] + tables[3])[None]
    input_grad = input_grad_of(z_at, clip_tokens, mark, back, modulation)
    new_fragment, new_momentum = outer_step(pseudo_grad[0], outer_params, outer_momentum)
    return (input_grad, weight_grad, table_grad, new_fragment, new_momentum)


def solution(mesh):
    grid = Mesh(mesh.devices.reshape(-1, SIDE, SIDE), ("rep", "zh", "xx"))
    fsdp = ("zh", "xx")
    every = ("rep", "zh", "xx")
    return jax.shard_map(
        shards,
        mesh=grid,
        in_specs=(
            P(every, None),
            P(every),
            P(),
            P(),
            P("rep", fsdp, None),
            P(every, None),
            P("rep", fsdp),
            P(fsdp),
            P(fsdp),
        ),
        out_specs=(
            P(every, None),
            P("rep", fsdp, None),
            P("rep", None, fsdp),
            P(fsdp),
            P(fsdp),
        ),
        check_vma=False,
    )
```

```python
import functools

import jax
import jax.numpy as jnp
from jax import lax
from jax.experimental import pallas as pl
from jax.experimental.pallas import tpu as pltpu
from jax.sharding import Mesh
from jax.sharding import PartitionSpec as P

EPSILON = 1e-06
OUTER_RATE = 0.7
OUTER_MOMENTUM = 0.9
WIDTHS = (1024, 1024, 1024)
SIDE = 4
LANES = 128
VMEM_BYTES = 16 * 1024 * 1024
F32 = jnp.float32
BF16 = jnp.bfloat16
PLACES = (0, 3, 1, 2)
NN = (((1,), (0,)), ((), ()))
NT = (((1,), (1,)), ((), ()))
TN = (((0,), (0,)), ((), ()))


def shift(value, axis, step):
    return lax.ppermute(value, axis, [(i, (i + step) % SIDE) for i in range(SIDE)])


def exchange(value, axis, bit):
    return lax.ppermute(value, axis, [(i, i ^ bit) for i in range(16)])


def call(kernel, outs, *operands, flops=0, fresh=()):
    size = sum(a.size * a.dtype.itemsize for a in operands) + sum(
        o.size * o.dtype.itemsize for o in outs
    )
    places = [
        pltpu.SMEM if a.ndim == 1 else pl.ANY if i in fresh else pltpu.VMEM
        for i, a in enumerate(operands)
    ]
    scratch = [pltpu.VMEM(operands[i].shape, operands[i].dtype) for i in fresh]
    if fresh:
        scratch.append(pltpu.SemaphoreType.DMA((len(fresh),)))

    def body(*refs):
        if not fresh:
            kernel(*refs)
            return
        refs, held, sems = refs[: -1 - len(fresh)], refs[-1 - len(fresh) : -1], refs[-1]
        refs = list(refs)
        copies = []
        for n, i in enumerate(fresh):
            copies.append(pltpu.make_async_copy(refs[i], held[n], sems.at[n]))
            refs[i] = held[n]
        for copy in copies:
            copy.start()
        for copy in copies:
            copy.wait()
        kernel(*refs)

    return pl.pallas_call(
        body,
        out_shape=outs,
        in_specs=[pl.BlockSpec(memory_space=place) for place in places],
        out_specs=[pl.BlockSpec(memory_space=pltpu.VMEM) for _ in outs],
        scratch_shapes=scratch,
        compiler_params=pltpu.CompilerParams(vmem_limit_bytes=VMEM_BYTES),
        cost_estimate=pl.CostEstimate(
            flops=flops // 8, bytes_accessed=size // 8, transcendentals=0
        ),
    )(*operands)


def shape(rows, columns, dtype):
    return jax.ShapeDtypeStruct((rows, columns), dtype)


def together(*groups):
    flat = lax.optimization_barrier(sum((tuple(g) for g in groups), ()))
    out = []
    for group in groups:
        out.append(list(flat[: len(group)]))
        flat = flat[len(group) :]
    return out


def both_ways(to_right, to_left, axis):
    return [shift(to_right, axis, 1), shift(to_left, axis, -1)]


def relay_sum(keep_r, keep_l, got):
    half, columns = keep_r.shape
    return call(
        relay_kernel,
        [shape(half, columns, BF16)] * 2,
        keep_r,
        got[0],
        keep_l,
        got[1],
        fresh=(1, 3),
    )


def pass_on(got, axis):
    half = got[0].shape[0] // 2
    return both_ways(got[0][:half], got[1][half:], axis)


def relay_kernel(keep_r, got_r, keep_l, got_l, out_r, out_l):
    half = keep_r.shape[0]
    out_r[...] = (keep_r[...] + got_r[:half, :].astype(F32)).astype(BF16)
    out_l[...] = (keep_l[...] + got_l[:half, :].astype(F32)).astype(BF16)


def split_out(blocks, own, message_r, message_l, keep_r, keep_l):
    half = keep_r.shape[0]
    own[...] = blocks[0]
    message_r[:half, :] = blocks[3][:half].astype(BF16)
    message_r[half:, :] = blocks[2][half:].astype(BF16)
    keep_r[...] = blocks[2][:half]
    message_l[:half, :] = blocks[3][half:].astype(BF16)
    message_l[half:, :] = blocks[1][:half].astype(BF16)
    keep_l[...] = blocks[1][half:]


def split_shapes(rows, columns):
    return [
        shape(rows, columns, F32),
        shape(rows, columns, BF16),
        shape(rows, columns, BF16),
        shape(rows // 2, columns, F32),
        shape(rows // 2, columns, F32),
    ]


def modulation_parts(modulation):
    high = modulation.astype(BF16)
    rest = modulation - high.astype(F32)
    middle = rest.astype(BF16)
    low = (rest - middle.astype(F32)).astype(BF16)
    return jnp.concatenate([high, middle, low], axis=0)


def hot(frame, copies, count):
    ids = frame.astype(jnp.int32)
    places = lax.broadcasted_iota(jnp.int32, (frame.shape[0], copies * count), 1)
    return jnp.where(lax.rem(places, count) == ids, 1.0, 0.0).astype(BF16)


def block_at(where, place, size):
    return pl.ds(pl.multiple_of(lax.rem(where[0] + place, SIDE) * size, 128), size)


def pack_kernel(where, tokens, ids, o0, o1, o2, o3, marks):
    part = o0.shape[1] - LANES
    square = tokens[...].astype(F32)
    inverse = lax.rsqrt(jnp.mean(square * square, axis=-1, keepdims=True) + EPSILON)
    rows = tokens.shape[0]
    frame = jnp.transpose(jnp.broadcast_to(ids[...].astype(F32), (LANES, rows)))
    lane = lax.broadcasted_iota(jnp.int32, (tokens.shape[0], LANES), 1)
    marks[...] = jnp.where(lane == 0, inverse, frame)
    high = inverse.astype(BF16).astype(F32)
    middle = (inverse - high).astype(BF16).astype(F32)
    low = inverse - high - middle
    packed = jnp.where(
        lane == 0, high, jnp.where(lane == 1, middle, jnp.where(lane == 2, low, frame))
    ).astype(BF16)
    for place, out in zip(PLACES, (o0, o1, o2, o3)):
        out[:, :part] = tokens[:, block_at(where, place, part)]
        out[:, part:] = packed


def unpack(piece, part):
    packed = piece[:, part:].astype(F32)
    inverse = packed[:, 0:1] + packed[:, 1:2] + packed[:, 2:3]
    return piece[:, :part].astype(F32) * inverse, packed[:, 3:4]


def prepare_kernel(p0, p1, p2, p3, modulation, out, kept):
    rows = p0.shape[0]
    part = out.shape[1]
    parts = modulation_parts(modulation[...])
    for i, piece in enumerate((p0, p1, p2, p3)):
        kept[i * rows : (i + 1) * rows, :] = piece[...]
        normed, frame = unpack(piece, part)
        frame_mod = jnp.dot(
            hot(frame, 3, modulation.shape[0]), parts, preferred_element_type=F32
        )
        out[i * rows : (i + 1) * rows, :] = (normed * (1.0 + frame_mod)).astype(BF16)


def project_kernel(normal_in, weight, *outs):
    total = jnp.dot(normal_in[...], weight[...], preferred_element_type=F32)
    rows = outs[0].shape[0]
    split_out([total[i * rows : (i + 1) * rows] for i in range(SIDE)], *outs)


def head_kernel(own, got_r, got_l, last_r, last_l, cotangent, gain, out):
    rows, columns = own.shape
    half = rows // 2
    head = gain.shape[1]
    for h in range(columns // head):
        span = slice(h * head, (h + 1) * head)
        for side in range(2):
            some = slice(side * half, (side + 1) * half)
            first, second = (last_r, got_l) if side == 0 else (last_l, got_r)
            at = (slice(0, half), slice(half, rows))
            projected = (
                own[some, span] + first[at[0], span].astype(F32) + second[at[1], span].astype(F32)
            )
            inverse = lax.rsqrt(
                jnp.mean(projected * projected, axis=-1, keepdims=True) + EPSILON
            )
            hat = projected * inverse
            scaled = cotangent[some, span].astype(F32) * gain[...]
            grad = inverse * (scaled - hat * jnp.mean(scaled * hat, axis=-1, keepdims=True))
            out[some, span] = grad.astype(BF16)


def normal_grad_kernel(g0, g1, g2, g3, g4, weight, *refs):
    *old, out = refs
    depth = weight.shape[0] // SIDE
    grad = jnp.concatenate([g0[...], g1[...], g2[...], g3[...], g4[...]], axis=0)
    for i in range(SIDE):
        span = slice(i * depth, (i + 1) * depth)
        term = lax.dot_general(grad, weight[span, :], NT, preferred_element_type=F32)
        out[:, span] = term + old[0][:, span] if old else term


def last_normal_grad_kernel(g0, g1, g2, g3, g4, weight, old, *outs):
    rows = g0.shape[0]
    depth = weight.shape[0] // SIDE
    grad = jnp.concatenate([g0[...], g1[...], g2[...], g3[...], g4[...]], axis=0)
    for i in range(SIDE):
        span = slice(i * depth, (i + 1) * depth)
        term = old[:, span] + lax.dot_general(
            grad, weight[span, :], NT, preferred_element_type=F32
        )
        for j in range(SIDE):
            outs[j][:, span] = term[j * rows : (j + 1) * rows].astype(BF16)


def weight_grad_whole_kernel(normal_in, g0, g1, g2, g3, g4, out, held, got, sems):
    pieces = (g0, g1, g2, g3, g4)
    copies = []
    start = 0
    for n, piece in enumerate(pieces):
        rows = piece.shape[0]
        copies.append(
            pltpu.make_async_copy(piece, got.at[pl.ds(start, rows)], sems.at[SIDE + n])
        )
        start += rows
    for copy in copies:
        copy.start()
    for copy in copies:
        copy.wait()
    depth = out.shape[0] // SIDE
    copies = []
    for i in range(SIDE):
        span = slice(i * depth, (i + 1) * depth)
        held[span, :] = lax.dot_general(
            normal_in[:, span], got[...], TN, preferred_element_type=F32
        ).astype(BF16)
        place = pl.ds(i * depth, depth)
        copies.append(pltpu.make_async_copy(held.at[place], out.at[place], sems.at[i]))
        copies[-1].start()
    for copy in copies:
        copy.wait()


def weight_grad_whole(normal_in, grads):
    rows, part = normal_in.shape
    step = grads[0].shape[1]
    return pl.pallas_call(
        weight_grad_whole_kernel,
        out_shape=shape(part, step, BF16),
        in_specs=[pl.BlockSpec(memory_space=pltpu.VMEM)]
        + [pl.BlockSpec(memory_space=pl.ANY)] * len(grads),
        out_specs=pl.BlockSpec(memory_space=pl.ANY),
        scratch_shapes=[
            pltpu.VMEM((part, step), BF16),
            pltpu.VMEM((rows, step), BF16),
            pltpu.SemaphoreType.DMA((SIDE + len(grads),)),
        ],
        compiler_params=pltpu.CompilerParams(vmem_limit_bytes=VMEM_BYTES),
        cost_estimate=pl.CostEstimate(
            flops=rows * part * step // 4, bytes_accessed=part * step // 4, transcendentals=0
        ),
    )(normal_in, *grads)


def table_kernel(where, n0, n1, n2, n3, pieces, o0, o1, o2, o3, total):
    count, depth = o0.shape
    rows = n0.shape[0]
    acc = None
    for i, grad in enumerate((n0, n1, n2, n3)):
        normed, frame = unpack(pieces[i * rows : (i + 1) * rows, :], grad.shape[1])
        product = grad[...].astype(F32) * normed
        high = product.astype(BF16)
        low = (product - high.astype(F32)).astype(BF16)
        one_hot = hot(frame, 1, count)
        term = lax.dot_general(one_hot, high, TN, preferred_element_type=F32)
        term = term + lax.dot_general(one_hot, low, TN, preferred_element_type=F32)
        acc = term if acc is None else acc + term
    total[...] = acc
    for place, out in zip(PLACES, (o0, o1, o2, o3)):
        out[...] = total[:, block_at(where, place, depth)]


def input_kernel(where, tokens, marks, b0, b1, b2, b3, modulation, out):
    part = b0.shape[1]
    mark = marks[...]
    inverse = mark[:, 0:1]
    one_hot = hot(mark[:, 1:2], 3, modulation.shape[0])
    places = (0, 1, 3, 2)

    def load(place, piece):
        span = block_at(where, place, part)
        frame_mod = jnp.dot(
            one_hot, modulation_parts(modulation[:, span]), preferred_element_type=F32
        )
        grad_hat = piece[...].astype(F32) * (1.0 + frame_mod)
        return span, grad_hat, tokens[:, span].astype(F32) * inverse

    total = 0.0
    for place, piece in zip(places, (b0, b1, b2, b3)):
        span, grad_hat, normed = load(place, piece)
        total = total + jnp.sum(grad_hat * normed, axis=-1, keepdims=True)
    mean = total / (part * SIDE)
    for place, piece in zip(places, (b0, b1, b2, b3)):
        span, grad_hat, normed = load(place, piece)
        out[:, span] = (inverse * (grad_hat - normed * mean)).astype(BF16)


def input_grad_of(where, tokens, marks, back, modulation):
    rows, width = tokens.shape
    part = width // SIDE
    tile = 32
    row_tile = lambda columns: pl.BlockSpec((tile, columns), lambda i: (i, 0))
    return pl.pallas_call(
        input_kernel,
        out_shape=shape(rows, width, BF16),
        grid=(rows // tile,),
        in_specs=[
            pl.BlockSpec(memory_space=pltpu.SMEM),
            row_tile(width),
            row_tile(LANES),
            row_tile(part),
            row_tile(part),
            row_tile(part),
            row_tile(part),
            pl.BlockSpec(modulation.shape, lambda i: (0, 0)),
        ],
        out_specs=row_tile(width),
        compiler_params=pltpu.CompilerParams(vmem_limit_bytes=VMEM_BYTES),
        cost_estimate=pl.CostEstimate(
            flops=rows * width * 12, bytes_accessed=rows * width * 6, transcendentals=0
        ),
    )(where, tokens, marks, *back, modulation)


def add_other(total, bit):
    wide = total.astype(F32) + exchange(total, "rep", bit).astype(F32)
    return wide, wide.astype(BF16)


def outer_step(total, outer_params, outer_momentum):
    average = total / 16
    new_momentum = OUTER_MOMENTUM * outer_momentum + average
    new_fragment = outer_params - OUTER_RATE * (average + OUTER_MOMENTUM * new_momentum)
    return new_fragment, new_momentum


def spread(pieces, axis):
    return [
        pieces[0],
        shift(pieces[1], axis, -1),
        shift(pieces[2], axis, 1),
        shift(pieces[3], axis, 2),
    ]


def shards(
    clip_tokens,
    frame_ids,
    modulation,
    query_gain,
    query_weight,
    query_cotangent,
    pseudo_grad,
    outer_params,
    outer_momentum,
):
    z = lax.axis_index("zh")
    z_at = z.astype(jnp.int32)[None]
    x_at = lax.axis_index("xx").astype(jnp.int32)[None]
    rows, width = clip_tokens.shape
    part = width // SIDE
    depth = part // SIDE
    gain = query_gain[None, :]

    *packed, mark = call(
        pack_kernel,
        [shape(rows, part + LANES, BF16)] * SIDE + [shape(rows, LANES, F32)],
        z_at,
        clip_tokens,
        frame_ids[None, :],
        fresh=(1,),
    )
    mine = query_weight[0]
    starts = [sum(WIDTHS[:c]) for c in range(len(WIDTHS))]
    weights = [
        lax.all_gather(mine[:, start : start + step], "xx", axis=0, tiled=True)
        for start, step in zip(starts, WIDTHS)
    ]
    packed, (x_at,) = together(packed, [x_at])
    got = spread(packed, "zh")
    group_mod = lax.dynamic_slice_in_dim(modulation, z * part, part, 1)
    normal_in, kept = call(
        prepare_kernel,
        [shape(SIDE * rows, part, BF16), shape(SIDE * rows, part + LANES, BF16)],
        got[0],
        got[2],
        got[1],
        got[3],
        group_mod,
    )
    total = pseudo_grad[0].astype(BF16)
    for bit in (1, 4):
        _, total = add_other(total, bit)
    (normal_in,), (total,) = together([normal_in], [total])

    normal_total = []
    row_grads = []
    for c, (start, step) in enumerate(zip(starts, WIDTHS)):
        matmul = 2 * SIDE * rows * part * step
        own, message_r, message_l, *keep = call(
            project_kernel, split_shapes(rows, step), normal_in, weights[c], flops=matmul
        )
        got = both_ways(message_r, message_l, "zh")
        if c > 0:
            for bit in (8, 2)[c - 1 : c]:
                wide, total = add_other(total, bit)
            whole = weight_grad_whole(normal_in, grads)
            got, (whole,), (wide, total) = together(got, [whole], [wide, total])
            row_grads.append(lax.psum_scatter(whole, "xx", scatter_dimension=0, tiled=True))
        if c == 2:
            outer = outer_step(wide, outer_params, outer_momentum)
        last = both_ways(*relay_sum(*keep, got), "zh")
        if c > 0:
            normal_total = call(
                normal_grad_kernel,
                [shape(SIDE * rows, part, F32)],
                *grads,
                weights[c - 1],
                *normal_total,
                flops=matmul,
            )
            last, normal_total = together(last, normal_total)
        (grad,) = call(
            head_kernel,
            [shape(rows, step, BF16)],
            own,
            *got,
            *last,
            query_cotangent[:, start : start + step],
            gain,
            fresh=(0, 1, 2, 3, 4, 5),
        )
        (grad,), (normal_in,) = together([grad], [normal_in])
        near = both_ways(grad, grad, "zh")
        grads = [grad, *near, *pass_on(near, "zh")]
    normal_total = call(
        last_normal_grad_kernel,
        [shape(rows, part, BF16)] * SIDE,
        *grads,
        weights[-1],
        *normal_total,
        flops=matmul,
        fresh=(1, 2, 3, 4),
    )
    normal_total, grads = together(normal_total, grads)
    back = spread(normal_total, "zh")
    whole = weight_grad_whole(normal_in, grads)
    last_grad = lax.psum_scatter(whole, "xx", scatter_dimension=0, tiled=True)
    weight_grad = jnp.concatenate(row_grads + [jnp.zeros_like(last_grad)], axis=1)
    back, (weight_grad,) = together(back, [weight_grad])
    weight_grad = lax.dynamic_update_slice(weight_grad, last_grad, (0, starts[-1]))
    *tables, _ = call(
        table_kernel,
        [shape(modulation.shape[0], depth, F32)] * SIDE + [shape(modulation.shape[0], part, F32)],
        x_at,
        *normal_total,
        kept,
    )
    tables = spread(tables, "xx")
    input_grad = input_grad_of(z_at, clip_tokens, mark, back, modulation)
    (input_grad,), tables = together([input_grad], tables)
    table_grad = (tables[0] + tables[1] + tables[2] + tables[3])[None]
    return (input_grad, weight_grad[None], table_grad, *outer)


def solution(mesh):
    grid = Mesh(mesh.devices.reshape(-1, SIDE, SIDE), ("rep", "zh", "xx"))
    fsdp = ("zh", "xx")
    every = ("rep", "zh", "xx")
    return jax.shard_map(
        shards,
        mesh=grid,
        in_specs=(
            P(every, None),
            P(every),
            P(),
            P(),
            P("rep", fsdp, None),
            P(every, None),
            P("rep", fsdp),
            P(fsdp),
            P(fsdp),
        ),
        out_specs=(
            P(every, None),
            P("rep", fsdp, None),
            P("rep", None, fsdp),
            P(fsdp),
            P(fsdp),
        ),
        check_vma=False,
    )
```

```python
import functools

import jax
import jax.numpy as jnp
from jax import lax
from jax.experimental import pallas as pl
from jax.experimental.pallas import tpu as pltpu
from jax.sharding import Mesh
from jax.sharding import PartitionSpec as P

EPSILON = 1e-06
OUTER_RATE = 0.7
OUTER_MOMENTUM = 0.9
WIDTHS = (1024, 1024, 1024)
SIDE = 4
LANES = 128
VMEM_BYTES = 16 * 1024 * 1024
F32 = jnp.float32
BF16 = jnp.bfloat16
PLACES = (0, 3, 1, 2)
NN = (((1,), (0,)), ((), ()))
NT = (((1,), (1,)), ((), ()))
TN = (((0,), (0,)), ((), ()))


def shift(value, axis, step):
    return lax.ppermute(value, axis, [(i, (i + step) % SIDE) for i in range(SIDE)])


def exchange(value, axis, bit):
    return lax.ppermute(value, axis, [(i, i ^ bit) for i in range(16)])


def call(kernel, outs, *operands, flops=0, fresh=()):
    size = sum(a.size * a.dtype.itemsize for a in operands) + sum(
        o.size * o.dtype.itemsize for o in outs
    )
    places = [
        pltpu.SMEM if a.ndim == 1 else pl.ANY if i in fresh else pltpu.VMEM
        for i, a in enumerate(operands)
    ]
    scratch = [pltpu.VMEM(operands[i].shape, operands[i].dtype) for i in fresh]
    if fresh:
        scratch.append(pltpu.SemaphoreType.DMA((len(fresh),)))

    def body(*refs):
        if not fresh:
            kernel(*refs)
            return
        refs, held, sems = refs[: -1 - len(fresh)], refs[-1 - len(fresh) : -1], refs[-1]
        refs = list(refs)
        copies = []
        for n, i in enumerate(fresh):
            copies.append(pltpu.make_async_copy(refs[i], held[n], sems.at[n]))
            refs[i] = held[n]
        for copy in copies:
            copy.start()
        for copy in copies:
            copy.wait()
        kernel(*refs)

    return pl.pallas_call(
        body,
        out_shape=outs,
        in_specs=[pl.BlockSpec(memory_space=place) for place in places],
        out_specs=[pl.BlockSpec(memory_space=pltpu.VMEM) for _ in outs],
        scratch_shapes=scratch,
        compiler_params=pltpu.CompilerParams(vmem_limit_bytes=VMEM_BYTES),
        cost_estimate=pl.CostEstimate(
            flops=flops // 8, bytes_accessed=size // 8, transcendentals=0
        ),
    )(*operands)


def shape(rows, columns, dtype):
    return jax.ShapeDtypeStruct((rows, columns), dtype)


def together(*groups):
    flat = lax.optimization_barrier(sum((tuple(g) for g in groups), ()))
    out = []
    for group in groups:
        out.append(list(flat[: len(group)]))
        flat = flat[len(group) :]
    return out


def both_ways(to_right, to_left, axis):
    return [shift(to_right, axis, 1), shift(to_left, axis, -1)]


def relay_sum(keep_r, keep_l, got):
    half, columns = keep_r.shape
    return call(
        relay_kernel,
        [shape(half, columns, BF16)] * 2,
        keep_r,
        got[0],
        keep_l,
        got[1],
        fresh=(1, 3),
    )


def pass_on(got, axis):
    half = got[0].shape[0] // 2
    return both_ways(got[0][:half], got[1][half:], axis)


def relay_kernel(keep_r, got_r, keep_l, got_l, out_r, out_l):
    half = keep_r.shape[0]
    out_r[...] = (keep_r[...] + got_r[:half, :].astype(F32)).astype(BF16)
    out_l[...] = (keep_l[...] + got_l[:half, :].astype(F32)).astype(BF16)


def split_out(blocks, own, message_r, message_l, keep_r, keep_l):
    half = keep_r.shape[0]
    own[...] = blocks[0]
    message_r[:half, :] = blocks[3][:half].astype(BF16)
    message_r[half:, :] = blocks[2][half:].astype(BF16)
    keep_r[...] = blocks[2][:half]
    message_l[:half, :] = blocks[3][half:].astype(BF16)
    message_l[half:, :] = blocks[1][:half].astype(BF16)
    keep_l[...] = blocks[1][half:]


def split_shapes(rows, columns):
    return [
        shape(rows, columns, F32),
        shape(rows, columns, BF16),
        shape(rows, columns, BF16),
        shape(rows // 2, columns, F32),
        shape(rows // 2, columns, F32),
    ]


def modulation_parts(modulation):
    high = modulation.astype(BF16)
    rest = modulation - high.astype(F32)
    middle = rest.astype(BF16)
    low = (rest - middle.astype(F32)).astype(BF16)
    return jnp.concatenate([high, middle, low], axis=0)


def hot(frame, copies, count):
    ids = frame.astype(jnp.int32)
    places = lax.broadcasted_iota(jnp.int32, (frame.shape[0], copies * count), 1)
    return jnp.where(lax.rem(places, count) == ids, 1.0, 0.0).astype(BF16)


def block_at(where, place, size):
    return pl.ds(pl.multiple_of(lax.rem(where[0] + place, SIDE) * size, 128), size)


def pack_kernel(where, tokens, ids, o0, o1, o2, o3, marks):
    part = o0.shape[1] - LANES
    square = tokens[...].astype(F32)
    inverse = lax.rsqrt(jnp.mean(square * square, axis=-1, keepdims=True) + EPSILON)
    rows = tokens.shape[0]
    frame = jnp.transpose(jnp.broadcast_to(ids[...].astype(F32), (LANES, rows)))
    lane = lax.broadcasted_iota(jnp.int32, (tokens.shape[0], LANES), 1)
    marks[...] = jnp.where(lane == 0, inverse, frame)
    high = inverse.astype(BF16).astype(F32)
    middle = (inverse - high).astype(BF16).astype(F32)
    low = inverse - high - middle
    packed = jnp.where(
        lane == 0, high, jnp.where(lane == 1, middle, jnp.where(lane == 2, low, frame))
    ).astype(BF16)
    for place, out in zip(PLACES, (o0, o1, o2, o3)):
        out[:, :part] = tokens[:, block_at(where, place, part)]
        out[:, part:] = packed


def unpack(piece, part):
    packed = piece[:, part:].astype(F32)
    inverse = packed[:, 0:1] + packed[:, 1:2] + packed[:, 2:3]
    return piece[:, :part].astype(F32) * inverse, packed[:, 3:4]


def prepare_kernel(p0, p1, p2, p3, modulation, out, kept):
    rows = p0.shape[0]
    part = out.shape[1]
    parts = modulation_parts(modulation[...])
    for i, piece in enumerate((p0, p1, p2, p3)):
        kept[i * rows : (i + 1) * rows, :] = piece[...]
        normed, frame = unpack(piece, part)
        frame_mod = jnp.dot(
            hot(frame, 3, modulation.shape[0]), parts, preferred_element_type=F32
        )
        out[i * rows : (i + 1) * rows, :] = (normed * (1.0 + frame_mod)).astype(BF16)


def project_kernel(normal_in, weight, *outs):
    total = jnp.dot(normal_in[...], weight[...], preferred_element_type=F32)
    rows = outs[0].shape[0]
    split_out([total[i * rows : (i + 1) * rows] for i in range(SIDE)], *outs)


def head_kernel(own, got_r, got_l, last_r, last_l, cotangent, gain, out):
    rows, columns = own.shape
    half = rows // 2
    head = gain.shape[1]
    for h in range(columns // head):
        span = slice(h * head, (h + 1) * head)
        for side in range(2):
            some = slice(side * half, (side + 1) * half)
            first, second = (last_r, got_l) if side == 0 else (last_l, got_r)
            at = (slice(0, half), slice(half, rows))
            projected = (
                own[some, span] + first[at[0], span].astype(F32) + second[at[1], span].astype(F32)
            )
            inverse = lax.rsqrt(
                jnp.mean(projected * projected, axis=-1, keepdims=True) + EPSILON
            )
            hat = projected * inverse
            scaled = cotangent[some, span].astype(F32) * gain[...]
            grad = inverse * (scaled - hat * jnp.mean(scaled * hat, axis=-1, keepdims=True))
            out[some, span] = grad.astype(BF16)


def normal_grad_kernel(g0, g1, g2, g3, g4, weight, *refs):
    *old, out = refs
    depth = weight.shape[0] // SIDE
    grad = jnp.concatenate([g0[...], g1[...], g2[...], g3[...], g4[...]], axis=0)
    for i in range(SIDE):
        span = slice(i * depth, (i + 1) * depth)
        term = lax.dot_general(grad, weight[span, :], NT, preferred_element_type=F32)
        out[:, span] = term + old[0][:, span] if old else term


def last_normal_grad_kernel(g0, g1, g2, g3, g4, weight, old, *outs):
    rows = g0.shape[0]
    depth = weight.shape[0] // SIDE
    grad = jnp.concatenate([g0[...], g1[...], g2[...], g3[...], g4[...]], axis=0)
    for i in range(SIDE):
        span = slice(i * depth, (i + 1) * depth)
        term = old[:, span] + lax.dot_general(
            grad, weight[span, :], NT, preferred_element_type=F32
        )
        for j in range(SIDE):
            outs[j][:, span] = term[j * rows : (j + 1) * rows].astype(BF16)


def weight_grad_whole_kernel(normal_in, g0, g1, g2, g3, g4, out, held, got, sems):
    pieces = (g0, g1, g2, g3, g4)
    copies = []
    start = 0
    for n, piece in enumerate(pieces):
        rows = piece.shape[0]
        copies.append(
            pltpu.make_async_copy(piece, got.at[pl.ds(start, rows)], sems.at[SIDE + n])
        )
        start += rows
    for copy in copies:
        copy.start()
    for copy in copies:
        copy.wait()
    depth = out.shape[0] // SIDE
    copies = []
    for i in range(SIDE):
        span = slice(i * depth, (i + 1) * depth)
        held[span, :] = lax.dot_general(
            normal_in[:, span], got[...], TN, preferred_element_type=F32
        ).astype(BF16)
        place = pl.ds(i * depth, depth)
        copies.append(pltpu.make_async_copy(held.at[place], out.at[place], sems.at[i]))
        copies[-1].start()
    for copy in copies:
        copy.wait()


def weight_grad_whole(normal_in, grads):
    rows, part = normal_in.shape
    step = grads[0].shape[1]
    return pl.pallas_call(
        weight_grad_whole_kernel,
        out_shape=shape(part, step, BF16),
        in_specs=[pl.BlockSpec(memory_space=pltpu.VMEM)]
        + [pl.BlockSpec(memory_space=pl.ANY)] * len(grads),
        out_specs=pl.BlockSpec(memory_space=pl.ANY),
        scratch_shapes=[
            pltpu.VMEM((part, step), BF16),
            pltpu.VMEM((rows, step), BF16),
            pltpu.SemaphoreType.DMA((SIDE + len(grads),)),
        ],
        compiler_params=pltpu.CompilerParams(vmem_limit_bytes=VMEM_BYTES),
        cost_estimate=pl.CostEstimate(
            flops=rows * part * step // 4, bytes_accessed=part * step // 4, transcendentals=0
        ),
    )(normal_in, *grads)


def table_kernel(where, n0, n1, n2, n3, pieces, o0, o1, o2, o3, total):
    count, depth = o0.shape
    rows = n0.shape[0]
    acc = None
    for i, grad in enumerate((n0, n1, n2, n3)):
        normed, frame = unpack(pieces[i * rows : (i + 1) * rows, :], grad.shape[1])
        product = grad[...].astype(F32) * normed
        high = product.astype(BF16)
        low = (product - high.astype(F32)).astype(BF16)
        one_hot = hot(frame, 1, count)
        term = lax.dot_general(one_hot, high, TN, preferred_element_type=F32)
        term = term + lax.dot_general(one_hot, low, TN, preferred_element_type=F32)
        acc = term if acc is None else acc + term
    total[...] = acc
    for place, out in zip(PLACES, (o0, o1, o2, o3)):
        out[...] = total[:, block_at(where, place, depth)]


def input_kernel(where, tokens, marks, b0, b1, b2, b3, modulation, out):
    part = b0.shape[1]
    mark = marks[...]
    inverse = mark[:, 0:1]
    one_hot = hot(mark[:, 1:2], 3, modulation.shape[0])
    places = (0, 1, 3, 2)

    def load(place, piece):
        span = block_at(where, place, part)
        frame_mod = jnp.dot(
            one_hot, modulation_parts(modulation[:, span]), preferred_element_type=F32
        )
        grad_hat = piece[...].astype(F32) * (1.0 + frame_mod)
        return span, grad_hat, tokens[:, span].astype(F32) * inverse

    total = 0.0
    for place, piece in zip(places, (b0, b1, b2, b3)):
        span, grad_hat, normed = load(place, piece)
        total = total + jnp.sum(grad_hat * normed, axis=-1, keepdims=True)
    mean = total / (part * SIDE)
    for place, piece in zip(places, (b0, b1, b2, b3)):
        span, grad_hat, normed = load(place, piece)
        out[:, span] = (inverse * (grad_hat - normed * mean)).astype(BF16)


def input_grad_of(where, tokens, marks, back, modulation):
    rows, width = tokens.shape
    part = width // SIDE
    tile = 32
    row_tile = lambda columns: pl.BlockSpec((tile, columns), lambda i: (i, 0))
    return pl.pallas_call(
        input_kernel,
        out_shape=shape(rows, width, BF16),
        grid=(rows // tile,),
        in_specs=[
            pl.BlockSpec(memory_space=pltpu.SMEM),
            row_tile(width),
            row_tile(LANES),
            row_tile(part),
            row_tile(part),
            row_tile(part),
            row_tile(part),
            pl.BlockSpec(modulation.shape, lambda i: (0, 0)),
        ],
        out_specs=row_tile(width),
        compiler_params=pltpu.CompilerParams(vmem_limit_bytes=VMEM_BYTES),
        cost_estimate=pl.CostEstimate(
            flops=rows * width * 12, bytes_accessed=rows * width * 6, transcendentals=0
        ),
    )(where, tokens, marks, *back, modulation)


def add_other(total, bit):
    wide = total.astype(F32) + exchange(total, "rep", bit).astype(F32)
    return wide, wide.astype(BF16)


def outer_step(total, outer_params, outer_momentum):
    average = total / 16
    new_momentum = OUTER_MOMENTUM * outer_momentum + average
    new_fragment = outer_params - OUTER_RATE * (average + OUTER_MOMENTUM * new_momentum)
    return new_fragment, new_momentum


def spread(pieces, axis):
    return [
        pieces[0],
        shift(pieces[1], axis, -1),
        shift(pieces[2], axis, 1),
        shift(pieces[3], axis, 2),
    ]


def shards(
    clip_tokens,
    frame_ids,
    modulation,
    query_gain,
    query_weight,
    query_cotangent,
    pseudo_grad,
    outer_params,
    outer_momentum,
):
    z = lax.axis_index("zh")
    z_at = z.astype(jnp.int32)[None]
    x_at = lax.axis_index("xx").astype(jnp.int32)[None]
    rows, width = clip_tokens.shape
    part = width // SIDE
    depth = part // SIDE
    gain = query_gain[None, :]

    *packed, mark = call(
        pack_kernel,
        [shape(rows, part + LANES, BF16)] * SIDE + [shape(rows, LANES, F32)],
        z_at,
        clip_tokens,
        frame_ids[None, :],
        fresh=(1,),
    )
    mine = query_weight[0]
    starts = [sum(WIDTHS[:c]) for c in range(len(WIDTHS))]
    weights = [
        lax.all_gather(mine[:, start : start + step], "xx", axis=0, tiled=True)
        for start, step in zip(starts, WIDTHS)
    ]
    group_mod = lax.dynamic_slice_in_dim(modulation, z * part, part, 1)
    packed, (x_at, group_mod) = together(packed, [x_at, group_mod])
    got = spread(packed, "zh")
    normal_in, kept = call(
        prepare_kernel,
        [shape(SIDE * rows, part, BF16), shape(SIDE * rows, part + LANES, BF16)],
        got[0],
        got[2],
        got[1],
        got[3],
        group_mod,
    )
    total = pseudo_grad[0].astype(BF16)
    for bit in (1, 4):
        _, total = add_other(total, bit)
    (normal_in,), (total,) = together([normal_in], [total])

    normal_total = []
    row_grads = []
    for c, (start, step) in enumerate(zip(starts, WIDTHS)):
        matmul = 2 * SIDE * rows * part * step
        own, message_r, message_l, *keep = call(
            project_kernel, split_shapes(rows, step), normal_in, weights[c], flops=matmul
        )
        got = both_ways(message_r, message_l, "zh")
        if c > 0:
            for bit in (8, 2)[c - 1 : c]:
                wide, total = add_other(total, bit)
            whole = weight_grad_whole(normal_in, grads)
            got, (whole,), (wide, total) = together(got, [whole], [wide, total])
            row_grads.append(lax.psum_scatter(whole, "xx", scatter_dimension=0, tiled=True))
        if c == 2:
            outer = outer_step(wide, outer_params, outer_momentum)
        last = both_ways(*relay_sum(*keep, got), "zh")
        if c > 0:
            normal_total = call(
                normal_grad_kernel,
                [shape(SIDE * rows, part, F32)],
                *grads,
                weights[c - 1],
                *normal_total,
                flops=matmul,
            )
            last, normal_total = together(last, normal_total)
        (grad,) = call(
            head_kernel,
            [shape(rows, step, BF16)],
            own,
            *got,
            *last,
            query_cotangent[:, start : start + step],
            gain,
            fresh=(0, 1, 2, 3, 4, 5),
        )
        (grad,), (normal_in,) = together([grad], [normal_in])
        near = both_ways(grad, grad, "zh")
        grads = [grad, *near, *pass_on(near, "zh")]
    normal_total = call(
        last_normal_grad_kernel,
        [shape(rows, part, BF16)] * SIDE,
        *grads,
        weights[-1],
        *normal_total,
        flops=matmul,
        fresh=(1, 2, 3, 4),
    )
    normal_total, grads = together(normal_total, grads)
    back = spread(normal_total, "zh")
    whole = weight_grad_whole(normal_in, grads)
    last_grad = lax.psum_scatter(whole, "xx", scatter_dimension=0, tiled=True)
    weight_grad = jnp.concatenate(row_grads + [jnp.zeros_like(last_grad)], axis=1)
    back, (weight_grad,) = together(back, [weight_grad])
    weight_grad = lax.dynamic_update_slice(weight_grad, last_grad, (0, starts[-1]))
    *tables, _ = call(
        table_kernel,
        [shape(modulation.shape[0], depth, F32)] * SIDE + [shape(modulation.shape[0], part, F32)],
        x_at,
        *normal_total,
        kept,
    )
    tables = spread(tables, "xx")
    input_grad = input_grad_of(z_at, clip_tokens, mark, back, modulation)
    (input_grad,), tables = together([input_grad], tables)
    table_grad = (tables[0] + tables[1] + tables[2] + tables[3])[None]
    return (input_grad, weight_grad[None], table_grad, *outer)


def solution(mesh):
    grid = Mesh(mesh.devices.reshape(-1, SIDE, SIDE), ("rep", "zh", "xx"))
    fsdp = ("zh", "xx")
    every = ("rep", "zh", "xx")
    return jax.shard_map(
        shards,
        mesh=grid,
        in_specs=(
            P(every, None),
            P(every),
            P(),
            P(),
            P("rep", fsdp, None),
            P(every, None),
            P("rep", fsdp),
            P(fsdp),
            P(fsdp),
        ),
        out_specs=(
            P(every, None),
            P("rep", fsdp, None),
            P("rep", None, fsdp),
            P(fsdp),
            P(fsdp),
        ),
        check_vma=False,
    )
```
